32 devices in a mesh: head: 2 (over core), req: 16 (over z, y, x).
Axes of the slice: x: 2, y: 2, z: 4, core: 2. Of those that a mesh axis runs over, the one named last changes fastest.
Arguments:
- queries: bfloat16 [128, 8192], P('req', 'head'), may hold values from -9 to 9
- new_key: bfloat16 [128, 1024], P('req', 'head'), may hold values from -4 to 4
- new_value: bfloat16 [128, 1024], P('req', 'head'), may hold values from -4 to 4
- key_cache: bfloat16 [1472, 64, 1024], P('req', None, 'head'), may hold values from -4 to 4
- value_cache: bfloat16 [1472, 64, 1024], P('req', None, 'head'), may hold values from -4 to 4
- lengths: int32 [128], P('req'), may hold values from 1 to 4096, as said below
- page_table: int32 [128, 64], P('req'), may hold values from 0 to 91, as said below
- residual: bfloat16 [128, 8192], P(None, ('head', 'req')), may hold values from -6 to 6
- out_weight: bfloat16 [8192, 8192], P(None, ('head', 'req')), may hold values from -0.25 to 0.25
- gate_weight: bfloat16 [8192, 28672], P('head', 'req'), may hold values from -0.0625 to 0.0625
- up_weight: bfloat16 [8192, 28672], P('head', 'req'), may hold values from -0.0625 to 0.0625
- down_weight: bfloat16 [28672, 8192], P('req', 'head'), may hold values from -0.046875 to 0.046875
Outputs:
- layer_out: bfloat16 [128, 8192], P(None, ('head', 'req'))
The draws below stay inside these ranges and needn't reach their ends.
Inputs may be any that keep to these rules, and one draw needn't show every extreme that they name: `lengths`: the 8 requests of one index of req hold at most one request of length 4096 and all others at most 256; each such group holds one request of length exactly 256, and some group holds one of length 4096. `page_table`: for request r the first ceil(lengths[r] / 64) entries name distinct pages of the pool of index r // 8 of req, and no page serves two requests; the other entries are arbitrary offsets and are not read.
All inputs are finite; a program needn't handle non-finite values.
Results may differ from the reference program's by a relative error of at most 0.01.
Values may be sent and summed in bfloat16 or wider, within the bound.
A program may use at most 192 MiB of HBM per device.

```python
import jax
import jax.numpy as jnp
from jax import lax

D = 8192
FF = 28672
QH = 64
KVH = 8
HD = 128
REQ_DEV = 8
PAGE = 64
LONG = 4096
SHORT = 256
PAGES_MAX = 64
POOL = 92
REQS = 128
N_REQ = 16


def draw_queries(key, part):
    sub_key = jax.random.fold_in(key, 21)
    base_draw = jnp.clip(jax.random.normal(sub_key, (REQS, QH * HD), jnp.float32), -4.0, 4.0)
    return base_draw.astype(jnp.bfloat16)


def draw_key_cache(key, part):
    rows_all = REQS // REQ_DEV * POOL
    sub_key = jax.random.fold_in(key, 41)
    base_draw = jnp.clip(jax.random.normal(sub_key, (rows_all, PAGE, KVH * HD), jnp.float32), -4.0, 4.0)
    return base_draw.astype(jnp.bfloat16)


def pool_order(sub_key):
    return jax.random.permutation(sub_key, POOL)


def pick_pages(permute, page_index):
    return permute[page_index]


def cache_layout(key):
    sub_keys = jax.random.split(jax.random.fold_in(key, 31), 6)
    devices = REQS // REQ_DEV
    chosen = jax.random.randint(sub_keys[0], (), 0, devices)
    has_long = (jax.random.randint(sub_keys[1], (devices,), 0, 5) < 2) | (jnp.arange(devices) == chosen)
    long_slot = jax.random.randint(sub_keys[2], (devices, 1), 0, REQ_DEV)
    short_slot = (long_slot + 1) % REQ_DEV
    slot_ids = jnp.arange(REQ_DEV).reshape(1, REQ_DEV)
    lengths = jax.random.randint(sub_keys[3], (devices, REQ_DEV), 1, SHORT + 1)
    lengths = jnp.where(slot_ids == short_slot, SHORT, lengths)
    lengths = jnp.where((slot_ids == long_slot) & has_long[:, None], LONG, lengths)
    used_pages = (lengths + PAGE - 1) // PAGE
    offsets = jnp.cumsum(used_pages, axis=1) - used_pages
    permutes = jax.vmap(pool_order)(jax.random.split(sub_keys[4], devices))
    slot_range = jnp.arange(PAGES_MAX).reshape(1, 1, PAGES_MAX)
    page_index = jnp.minimum(offsets[:, :, None] + slot_range, POOL - 1)
    live_pages = jax.vmap(pick_pages)(permutes, page_index)
    filler = jax.random.randint(sub_keys[5], (devices, REQ_DEV, PAGES_MAX), 0, POOL)
    table_out = jnp.where(slot_range < used_pages[:, :, None], live_pages, filler)
    return (lengths.reshape(REQS).astype(jnp.int32), table_out.reshape(REQS, PAGES_MAX).astype(jnp.int32))


def draw_lengths(key, part):
    return cache_layout(key)[0]


def draw_page_table(key, part):
    return cache_layout(key)[1]


def raised(drawn, own_key, source, target, blocks, factor):
    def block_of(axis_at):
        return (jnp.arange(drawn.shape[axis_at]) // (drawn.shape[axis_at] // blocks)).reshape((-1,) + (1,) * (drawn.ndim - 1 - axis_at))

    first = jax.random.permutation(own_key, blocks)[block_of(target)]
    other_side = (block_of(target) + blocks // 2) % blocks
    return jnp.where((block_of(source) == first) | (block_of(source) == other_side), factor * drawn, drawn)


def block_scale(key, dims, cuts, low, largest):
    loudness, own = 1.0, jax.random.fold_in(key, 6)
    for position, shards_of in cuts:
        steps = jnp.exp(jax.random.uniform(jax.random.fold_in(own, position), (shards_of,), jnp.float32, low / len(cuts), largest / len(cuts)))
        loudness = loudness * jnp.repeat(steps, dims[position] // shards_of).reshape([-1 if axis == position else 1 for axis in range(len(dims))])
    return loudness


def centred(key, extent, deviation, reach, cuts=(), held_as=jnp.bfloat16):
    result = deviation * jax.random.normal(key, extent, jnp.float32)
    if cuts:
        result = result * block_scale(key, extent, cuts, -0.22, 0.18)
    return jnp.clip(result, -reach, reach).astype(held_as)


def gaussian_with(stream_key, dims, deviation, limit, cuts, heavy, kind=jnp.bfloat16):
    drawn = deviation * jax.random.normal(stream_key, dims, jnp.float32)
    if cuts:
        drawn = drawn * block_scale(stream_key, dims, cuts, -0.22, 0.18)
    return jnp.clip(raised(drawn, jax.random.fold_in(stream_key, 3), *heavy), -limit, limit).astype(kind)


def setup_inputs(seed: int = 0) -> dict:
    arg_keys = jax.random.split(jax.random.key(seed), 13)
    return {
        "queries": draw_queries(jax.random.fold_in(arg_keys[12], 71), 0),
        "new_key": centred(arg_keys[1], (REQS, KVH * HD), 1.0, 4.0, ((0, 16), (1, 2))),
        "new_value": centred(arg_keys[2], (REQS, KVH * HD), 1.0, 4.0, ((0, 16), (1, 2))),
        "key_cache": draw_key_cache(jax.random.fold_in(arg_keys[12], 71), 0),
        "value_cache": centred(arg_keys[4], (N_REQ * POOL, PAGE, KVH * HD), 1.0, 4.0, ((0, 16), (2, 2))),
        "lengths": draw_lengths(jax.random.fold_in(arg_keys[12], 71), 0),
        "page_table": draw_page_table(jax.random.fold_in(arg_keys[12], 71), 0),
        "residual": centred(arg_keys[7], (REQS, D), 1.0, 6.0, ((1, 32),)),
        "out_weight": centred(arg_keys[8], (QH * HD, D), (4 * HD) ** -0.5, 0.25, ((1, 32),)),
        "gate_weight": centred(arg_keys[9], (D, FF), D ** -0.5, 0.0625, ((0, 2), (1, 16))),
        "up_weight": centred(arg_keys[10], (D, FF), D ** -0.5, 0.0625, ((0, 2), (1, 16))),
        "down_weight": gaussian_with(arg_keys[11], (FF, D), FF ** -0.5, 0.046875, ((0, 16), (1, 2)), (0, 1, 16, 2.0)),
    }


def attend_each(request_item, key_cache, value_cache):
    query_row, key_new, value_new, length, pages = request_item
    key_rows = key_cache[pages].reshape(-1, KVH, HD).astype(jnp.float32)
    value_rows = value_cache[pages].reshape(-1, KVH, HD).astype(jnp.float32)
    grouped = query_row.reshape(KVH, QH // KVH, HD).astype(jnp.float32)
    scores = jnp.einsum('gqd,tgd->gqt', grouped, key_rows) * HD ** -0.5
    own_score = jnp.einsum('gqd,gd->gq', grouped, key_new.reshape(KVH, HD).astype(jnp.float32)) * HD ** -0.5
    live_mask = (jnp.arange(key_rows.shape[0]).astype(jnp.int32) < length)[None, None, :]
    top_score = jnp.maximum(jnp.max(jnp.where(live_mask, scores, -1e30), axis=2), own_score)
    exp_terms = jnp.where(live_mask, jnp.exp(scores - top_score[:, :, None]), 0.0)
    own_exp = jnp.exp(own_score - top_score)
    total_mass = jnp.sum(exp_terms, axis=2) + own_exp
    weights = (exp_terms / total_mass[:, :, None]).astype(jnp.bfloat16)
    own_weight = (own_exp / total_mass).astype(jnp.bfloat16)
    summed = jnp.einsum('gqt,tgd->gqd', weights.astype(jnp.float32), value_rows)
    summed = summed + own_weight.astype(jnp.float32)[:, :, None] * value_new.reshape(KVH, 1, HD).astype(jnp.float32)
    return summed.reshape(-1).astype(jnp.bfloat16)


def reference(queries, new_key, new_value, key_cache, value_cache, lengths, page_table, residual, out_weight, gate_weight, up_weight, down_weight):
    owner_base = (jnp.arange(REQS).astype(jnp.int32) // REQ_DEV * POOL).astype(jnp.int32)
    pages = (page_table + owner_base[:, None]).astype(jnp.int32)

    def attend_request(request_item):
        return attend_each(request_item, key_cache, value_cache)

    attention = lax.map(attend_request, (queries, new_key, new_value, lengths, pages))
    mixed = (residual.astype(jnp.float32) + jnp.dot(attention, out_weight, preferred_element_type=jnp.float32)).astype(jnp.bfloat16)
    gate_acts = jnp.dot(mixed, gate_weight, preferred_element_type=jnp.float32)
    up_acts = jnp.dot(mixed, up_weight, preferred_element_type=jnp.float32)
    hidden = (jax.nn.silu(gate_acts) * up_acts).astype(jnp.bfloat16)
    down_part = jnp.dot(hidden, down_weight, preferred_element_type=jnp.float32)
    return (mixed.astype(jnp.float32) + down_part).astype(jnp.bfloat16)
```

```python
import functools

import jax
import jax.numpy as jnp
from jax import lax
from jax.experimental import pallas as pl
from jax.experimental.pallas import tpu as pltpu
from jax.sharding import PartitionSpec as P

HD = 128
MESH = pl.DeviceIdType.MESH
F32, BF16 = jnp.float32, jnp.bfloat16
NT = (((1,), (1,)), ((), ()))


def attend_kernel(
    short_pages, lengths, table, q_ref, nk_ref, nv_ref, keys, values, out_ref,
    ks, vs, kl, vl, s_ref, sl_ref, o_ref, sems,
):
    reqs, slots = table.shape
    page = keys.shape[1]
    groups = nk_ref.shape[0] // reqs
    per = q_ref.shape[0] // nk_ref.shape[0]
    span = short_pages * page
    block = groups * per
    scale = HD ** -0.5

    def start_short(r, carry):
        for i in range(short_pages):
            p = table[r, i]
            pltpu.make_async_copy(keys.at[p], ks.at[r, i], sems.at[0]).start()
            pltpu.make_async_copy(values.at[p], vs.at[r, i], sems.at[1]).start()
        return carry

    lax.fori_loop(0, reqs, start_short, 0)
    long_r = jnp.int32(-1)
    for r in range(reqs):
        long_r = jnp.where(lengths[r] > span, jnp.int32(r), long_r)
    has_long = long_r >= 0
    row = jnp.maximum(long_r, 0)

    @pl.when(has_long)
    def _():
        def start_long(i, carry):
            p = table[row, i]
            pltpu.make_async_copy(keys.at[p], kl.at[i], sems.at[2]).start()
            pltpu.make_async_copy(values.at[p], vl.at[i], sems.at[3]).start()
            return carry

        lax.fori_loop(0, slots, start_long, 0)

    def spread(ref):
        v = ref[...]
        return jnp.broadcast_to(v[:, None, :], (reqs * groups, per, HD)).reshape(-1, HD)

    q = q_ref[...]
    own = jnp.sum(q * spread(nk_ref), axis=1, keepdims=True) * scale
    new_v = spread(nv_ref)
    o_ref[...] = own * jnp.ones((1, HD), F32)

    pltpu.make_async_copy(ks, ks, sems.at[0]).wait()
    for r in range(reqs):
        for g in range(groups):
            at = r * block + g * per
            k = ks[r, :, :, g * HD:(g + 1) * HD].reshape(span, HD)
            s_ref[at:at + per, :] = lax.dot_general(
                q_ref[at:at + per, :].astype(BF16), k, NT, preferred_element_type=F32
            ) * scale
    pltpu.make_async_copy(vs, vs, sems.at[1]).wait()
    pos = lax.broadcasted_iota(jnp.int32, (block, span), 1)
    for r in range(reqs):
        rows = slice(r * block, (r + 1) * block)
        live = pos < lengths[r]
        s = jnp.where(live, s_ref[rows, :], -1e30)
        mine = own[rows]
        top = jnp.maximum(jnp.max(s, axis=1, keepdims=True), mine)
        e = jnp.where(live, jnp.exp(s - top), 0.0)
        own_e = jnp.exp(mine - top)
        inv = 1.0 / (jnp.sum(e, axis=1, keepdims=True) + own_e)
        s_ref[rows, :] = e * inv
        o_ref[rows, :] = (own_e * inv).astype(BF16).astype(F32) * new_v[rows]
    for r in range(reqs):
        for g in range(groups):
            at = r * block + g * per
            v = vs[r, :, :, g * HD:(g + 1) * HD].reshape(span, HD)
            o_ref[at:at + per, :] += jnp.dot(
                s_ref[at:at + per, :].astype(BF16), v, preferred_element_type=F32
            )

    @pl.when(has_long)
    def _():
        full = slots * page
        base = pl.multiple_of(row * block, block)
        pltpu.make_async_copy(kl, kl, sems.at[2]).wait()
        ql = q_ref[pl.ds(base, block), :]
        for g in range(groups):
            k = kl[:, :, g * HD:(g + 1) * HD].reshape(full, HD)
            sl_ref[g * per:(g + 1) * per, :] = lax.dot_general(
                ql[g * per:(g + 1) * per].astype(BF16), k, NT, preferred_element_type=F32
            ) * scale
        nkl = nk_ref[pl.ds(row * groups, groups), :]
        nvl = nv_ref[pl.ds(row * groups, groups), :]
        nkl = jnp.broadcast_to(nkl[:, None, :], (groups, per, HD)).reshape(block, HD)
        nvl = jnp.broadcast_to(nvl[:, None, :], (groups, per, HD)).reshape(block, HD)
        mine = jnp.sum(ql * nkl, axis=1, keepdims=True) * scale
        live = lax.broadcasted_iota(jnp.int32, (block, full), 1) < lengths[row]
        s = jnp.where(live, sl_ref[...], -1e30)
        top = jnp.maximum(jnp.max(s, axis=1, keepdims=True), mine)
        e = jnp.where(live, jnp.exp(s - top), 0.0)
        own_e = jnp.exp(mine - top)
        inv = 1.0 / (jnp.sum(e, axis=1, keepdims=True) + own_e)
        sl_ref[...] = e * inv
        added = (own_e * inv).astype(BF16).astype(F32) * nvl
        pltpu.make_async_copy(vl, vl, sems.at[3]).wait()
        parts = []
        for g in range(groups):
            v = vl[:, :, g * HD:(g + 1) * HD].reshape(full, HD)
            parts.append(jnp.dot(
                sl_ref[g * per:(g + 1) * per, :].astype(BF16), v, preferred_element_type=F32
            ))
        o_ref[pl.ds(base, block), :] = jnp.concatenate(parts, axis=0) + added

    out_ref[...] = o_ref[...].astype(BF16)


def attend(queries, new_key, new_value, keys, values, lengths, table):
    reqs, slots = table.shape
    _, page, width = keys.shape
    groups = width // HD
    short = min(4, slots)
    rows = queries.shape[1] // HD * reqs
    per_req = rows // reqs
    smem = pl.BlockSpec(memory_space=pltpu.SMEM)
    vmem = pl.BlockSpec(memory_space=pltpu.VMEM)
    hbm = pl.BlockSpec(memory_space=pl.ANY)
    out = pl.pallas_call(
        functools.partial(attend_kernel, short),
        out_shape=jax.ShapeDtypeStruct((rows, HD), BF16),
        in_specs=[smem, smem, vmem, vmem, vmem, hbm, hbm],
        out_specs=vmem,
        scratch_shapes=[
            pltpu.VMEM((reqs, short, page, width), BF16),
            pltpu.VMEM((reqs, short, page, width), BF16),
            pltpu.VMEM((slots, page, width), BF16),
            pltpu.VMEM((slots, page, width), BF16),
            pltpu.VMEM((rows, short * page), F32),
            pltpu.VMEM((per_req, slots * page), F32),
            pltpu.VMEM((rows, HD), F32),
            pltpu.SemaphoreType.DMA((4,)),
        ],
        compiler_params=pltpu.CompilerParams(vmem_limit_bytes=40 * 2**20),
        name="attend",
    )(
        lengths, table,
        queries.astype(F32).reshape(rows, HD),
        new_key.astype(F32).reshape(reqs * groups, HD),
        new_value.astype(F32).reshape(reqs * groups, HD),
        keys, values,
    )
    half = per_req // 2
    return out.reshape(reqs, 2, half, HD).transpose(1, 0, 2, 3).reshape(2 * reqs, half * HD)


def layer_kernel(
    A, B, att_ref, res_ref, wo_hbm, wg_hbm, wu_hbm, wd_hbm, out_ref,
    wo, wg, wu, wd, att, mix, acc_g, acc_u, xs, xr, hid, pf, ps, r1, zs, r2,
    wsem, sa, ra, sb, rb, ss, rs, sma, rma, smb, rmb, sx, rx, s1, g1, s2, g2,
):
    h = lax.axis_index("head")
    idx = lax.axis_index("req")
    a, b = idx // B, lax.rem(idx, B)
    n = A * B
    rows, c = res_ref.shape
    reqs = att_ref.shape[0] // 2
    kh = att_ref.shape[1]
    tiles, _, tile = acc_g.shape

    def far(da):
        return {"req": lax.rem(a + da, A) * B + b}

    def near(db):
        return {"req": a * B + lax.rem(b + db, B)}

    sibling = {"head": 1 - h}

    loads = [
        pltpu.make_async_copy(x, y, wsem.at[i])
        for i, (x, y) in enumerate(((wo_hbm, wo), (wg_hbm, wg), (wu_hbm, wu), (wd_hbm, wd)))
    ]
    for l in loads:
        l.start()

    barrier = pltpu.get_barrier_semaphore()
    for peer in [far(i) for i in range(1, A)] + [near(i) for i in range(1, B)] + [sibling]:
        pl.semaphore_signal(barrier, inc=1, device_id=peer, device_id_type=MESH)
    att[0, idx] = att_ref[...]
    pl.semaphore_wait(barrier, A + B - 1)

    def send(src, dst, s, r, to):
        cp = pltpu.make_async_remote_copy(
            src_ref=src, dst_ref=dst, send_sem=s, recv_sem=r, device_id=to, device_id_type=MESH
        )
        cp.start()
        return cp

    def source(da, db):
        return lax.rem(a + A - da, A) * B + lax.rem(b + B - db, B)

    def gather_start(ref, sfar, rfar, snear, rnear, each):
        fars = [None] + [
            send(ref.at[idx], ref.at[idx], sfar.at[d], rfar.at[d], far(d)) for d in range(1, A)
        ]
        nears = {}
        for da in range(A):
            if da:
                fars[da].wait_recv()
            at = source(da, 0)
            for db in range(1, B):
                nears[da, db] = send(
                    ref.at[at], ref.at[at], snear.at[da, db], rnear.at[da, db], near(db)
                )
            each(da, at)
        return fars, nears

    forwards = {}

    def forward(da, db, at):
        forwards[da, db] = send(
            att.at[0, at], att.at[1, at], ss.at[da, db], rs.at[da, db], sibling
        )

    fars, nears = gather_start(
        att.at[0], sa, ra, sb, rb, lambda da, at: forward(da, 0, at)
    )
    for da in range(A):
        for db in range(1, B):
            nears[da, db].wait_recv()
            forward(da, db, source(da, db))

    loads[0].wait()

    def project(slot, side):
        total = None
        lhs = att[slot].reshape(n * 2 * reqs, kh)
        for j in range(2):
            w = wo[pl.ds(pl.multiple_of((side * 2 + j) * kh, kh), kh), :]
            r = jnp.dot(lhs, w, preferred_element_type=F32)
            r = r.reshape(n, 2 * reqs, c)[:, j * reqs:(j + 1) * reqs].reshape(n * reqs, c)
            total = r if total is None else total + r
        return total

    update = project(0, h)
    for cp in forwards.values():
        cp.wait_recv()
    update = update + project(1, 1 - h)
    mix[idx] = (res_ref[...].astype(F32) + update).astype(BF16)

    mfars = [None] + [
        send(mix.at[idx], mix.at[idx], sma.at[d], rma.at[d], far(d)) for d in range(1, A)
    ]
    mnears = {}

    def spread(da):
        if da:
            mfars[da].wait_recv()
        at = source(da, 0)
        for db in range(1, B):
            mnears[da, db] = send(
                mix.at[at], mix.at[at], smb.at[da, db], rmb.at[da, db], near(db)
            )

    spread(0)
    loads[1].wait()
    loads[2].wait()
    for da in range(A):
        for db in range(1, B):
            mnears[da, db].wait_recv()
        if da + 1 < A:
            spread(da + 1)
        group = lax.rem(a + A - da, A) * B

        def do_tile(t, carry, da=da, group=group):
            cols = pl.ds(pl.multiple_of(t * tile, tile), tile) if tiles > 1 else slice(None)
            g = u = None
            for k in range(B):
                lhs = mix[group + k]
                at = pl.ds(pl.multiple_of((group + k) * c, c), c)
                gk = jnp.dot(lhs, wg[at, cols], preferred_element_type=F32)
                uk = jnp.dot(lhs, wu[at, cols], preferred_element_type=F32)
                g = gk if g is None else g + gk
                u = uk if u is None else u + uk
            if da:
                g = g + acc_g[t]
                u = u + acc_u[t]
            acc_g[t] = g
            acc_u[t] = u
            if da == A - 1:
                xs[t, 0] = g.astype(BF16)
                xs[t, 1] = u.astype(BF16)
                send(xs.at[t], xr.at[t], sx.at[t], rx.at[t], sibling)
            return carry

        lax.fori_loop(0, tiles, do_tile, 0)

    for t in range(tiles):
        pltpu.make_async_remote_copy(
            src_ref=xs.at[t], dst_ref=xr.at[t], send_sem=sx.at[t], recv_sem=rx.at[t],
            device_id=sibling, device_id_type=MESH,
        ).wait()
        g = acc_g[t] + xr[t, 0].astype(F32)
        u = acc_u[t] + xr[t, 1].astype(F32)
        hid[:, t * tile:(t + 1) * tile] = (g / (1.0 + jnp.exp(-g)) * u).astype(BF16)

    loads[3].wait()
    width = max(c, min(256, B * c))
    inner = width // c
    firsts, seconds = {}, []

    def reduce(i):
        total = pf[i % 2, b]
        for db in range(1, B):
            firsts[i, db].wait_recv()
            total = total + r1[i, db].astype(F32)
        return total

    def pass_on(i):
        zs[i] = reduce(i).astype(BF16)
        seconds.append(send(zs.at[i], r2.at[i], s2.at[i], g2.at[i], far(i + 1)))

    for i in range(A):
        ta = lax.rem(a + 1 + i, A)

        def do_cols(k, carry, i=i, ta=ta):
            cols = pl.ds(pl.multiple_of(ta * (B * c) + k * width, width), width)
            r = jnp.dot(hid[...], wd[:, cols], preferred_element_type=F32)
            for m in range(inner):
                piece = r[:, m * c:(m + 1) * c]
                pf[i % 2, k * inner + m] = piece
                ps[i, k * inner + m] = piece.astype(BF16)
            return carry

        lax.fori_loop(0, B // inner, do_cols, 0)
        for db in range(1, B):
            firsts[i, db] = send(
                ps.at[i, lax.rem(b + db, B)], r1.at[i, db], s1.at[i, db], g1.at[i, db], near(db)
            )
        if i:
            pass_on(i - 1)
    total = mix[idx].astype(F32) + reduce(A - 1)
    for i, cp in enumerate(seconds):
        cp.wait_recv()
        total = total + r2[i].astype(F32)
    out_ref[...] = total.astype(BF16)

    for cp in (
        fars[1:] + list(nears.values()) + list(forwards.values()) + mfars[1:]
        + list(mnears.values()) + list(firsts.values()) + seconds
    ):
        cp.wait_send()


def layer(n, att, residual, wo, wg, wu, wd):
    A = 4 if n % 4 == 0 else 1
    B = n // A
    rows, c = residual.shape
    ff = wg.shape[1]
    tile = 256 if ff % 256 == 0 else ff
    tiles = ff // tile
    vmem = pl.BlockSpec(memory_space=pltpu.VMEM)
    hbm = pl.BlockSpec(memory_space=pl.ANY)
    dma = pltpu.SemaphoreType.DMA
    return pl.pallas_call(
        functools.partial(layer_kernel, A, B),
        out_shape=jax.ShapeDtypeStruct((rows, c), BF16),
        in_specs=[vmem, vmem, hbm, hbm, hbm, hbm],
        out_specs=vmem,
        scratch_shapes=[
            pltpu.VMEM(wo.shape, BF16),
            pltpu.VMEM(wg.shape, BF16),
            pltpu.VMEM(wu.shape, BF16),
            pltpu.VMEM(wd.shape, BF16),
            pltpu.VMEM((2, n) + att.shape, BF16),
            pltpu.VMEM((n, rows, c), BF16),
            pltpu.VMEM((tiles, rows, tile), F32),
            pltpu.VMEM((tiles, rows, tile), F32),
            pltpu.VMEM((tiles, 2, rows, tile), BF16),
            pltpu.VMEM((tiles, 2, rows, tile), BF16),
            pltpu.VMEM((rows, ff), BF16),
            pltpu.VMEM((2, B, rows, c), F32),
            pltpu.VMEM((A, B, rows, c), BF16),
            pltpu.VMEM((A, B, rows, c), BF16),
            pltpu.VMEM((A, rows, c), BF16),
            pltpu.VMEM((A, rows, c), BF16),
            dma((4,)),
            dma((A,)), dma((A,)), dma((A, B)), dma((A, B)), dma((A, B)), dma((A, B)),
            dma((A,)), dma((A,)), dma((A, B)), dma((A, B)),
            dma((tiles,)), dma((tiles,)),
            dma((A, B)), dma((A, B)), dma((A,)), dma((A,)),
        ],
        compiler_params=pltpu.CompilerParams(
            vmem_limit_bytes=63 * 2**20, collective_id=0, has_side_effects=True
        ),
        name="layer",
    )(att, residual, wo, wg, wu, wd)


def solution(mesh):
    n = mesh.shape["req"]

    def body(
        queries, new_key, new_value, key_cache, value_cache, lengths, page_table,
        residual, out_weight, gate_weight, up_weight, down_weight,
    ):
        att = attend(queries, new_key, new_value, key_cache, value_cache, lengths, page_table)
        return layer(n, att, residual, out_weight, gate_weight, up_weight, down_weight)

    return jax.shard_map(
        body,
        mesh=mesh,
        in_specs=(
            P("req", "head"),
            P("req", "head"),
            P("req", "head"),
            P("req", None, "head"),
            P("req", None, "head"),
            P("req"),
            P("req", None),
            P(None, ("head", "req")),
            P(None, ("head", "req")),
            P("head", "req"),
            P("head", "req"),
            P("req", "head"),
        ),
        out_specs=P(None, ("head", "req")),
        check_vma=False,
    )
```

```python
import functools

import jax
import jax.numpy as jnp
from jax import lax
from jax.experimental import pallas as pl
from jax.experimental.pallas import tpu as pltpu
from jax.sharding import PartitionSpec as P

HD = 128
MESH = pl.DeviceIdType.MESH
F32, BF16 = jnp.float32, jnp.bfloat16
NT = (((1,), (1,)), ((), ()))


def attend_kernel(
    short_pages, lengths, table, q_in, nk_in, nv_in, keys, values, out_ref,
    q_ref, nk_ref, nv_ref, ks, vs, kl, vl, s_ref, sl_ref, o_ref, sems,
):
    reqs, slots = table.shape
    page = keys.shape[1]
    groups = nk_ref.shape[0] // reqs
    per = q_ref.shape[0] // nk_ref.shape[0]
    span = short_pages * page
    block = groups * per
    scale = HD ** -0.5

    def start_short(r, carry):
        for i in range(short_pages):
            p = table[r, i]
            pltpu.make_async_copy(keys.at[p], ks.at[r, i], sems.at[0]).start()
            pltpu.make_async_copy(values.at[p], vs.at[r, i], sems.at[1]).start()
        return carry

    lax.fori_loop(0, reqs, start_short, 0)
    long_r = jnp.int32(-1)
    for r in range(reqs):
        long_r = jnp.where(lengths[r] > span, jnp.int32(r), long_r)
    has_long = long_r >= 0
    row = jnp.maximum(long_r, 0)

    @pl.when(has_long)
    def _():
        def start_long(i, carry):
            p = table[row, i]
            pltpu.make_async_copy(keys.at[p], kl.at[i], sems.at[2]).start()
            pltpu.make_async_copy(values.at[p], vl.at[i], sems.at[3]).start()
            return carry

        lax.fori_loop(0, slots, start_long, 0)

    heads = groups * per
    for src, dst, count in ((q_in, q_ref, heads), (nk_in, nk_ref, groups), (nv_in, nv_ref, groups)):
        for i in range(count):
            dst[pl.ds(i, reqs, stride=count), :] = src[:, i * HD:(i + 1) * HD].astype(F32)

    def spread(ref):
        v = ref[...]
        return jnp.broadcast_to(v[:, None, :], (reqs * groups, per, HD)).reshape(-1, HD)

    q = q_ref[...]
    own = jnp.sum(q * spread(nk_ref), axis=1, keepdims=True) * scale
    new_v = spread(nv_ref)
    o_ref[...] = own * jnp.ones((1, HD), F32)

    pltpu.make_async_copy(ks, ks, sems.at[0]).wait()
    for r in range(reqs):
        for g in range(groups):
            at = r * block + g * per
            k = ks[r, :, :, g * HD:(g + 1) * HD].reshape(span, HD)
            s_ref[at:at + per, :] = lax.dot_general(
                q_ref[at:at + per, :].astype(BF16), k, NT, preferred_element_type=F32
            ) * scale
    pltpu.make_async_copy(vs, vs, sems.at[1]).wait()
    pos = lax.broadcasted_iota(jnp.int32, (block, span), 1)
    for r in range(reqs):
        rows = slice(r * block, (r + 1) * block)
        live = pos < lengths[r]
        s = jnp.where(live, s_ref[rows, :], -1e30)
        mine = own[rows]
        top = jnp.maximum(jnp.max(s, axis=1, keepdims=True), mine)
        e = jnp.where(live, jnp.exp(s - top), 0.0)
        own_e = jnp.exp(mine - top)
        inv = 1.0 / (jnp.sum(e, axis=1, keepdims=True) + own_e)
        s_ref[rows, :] = e * inv
        o_ref[rows, :] = (own_e * inv).astype(BF16).astype(F32) * new_v[rows]
    for r in range(reqs):
        for g in range(groups):
            at = r * block + g * per
            v = vs[r, :, :, g * HD:(g + 1) * HD].reshape(span, HD)
            o_ref[at:at + per, :] += jnp.dot(
                s_ref[at:at + per, :].astype(BF16), v, preferred_element_type=F32
            )

    @pl.when(has_long)
    def _():
        full = slots * page
        base = pl.multiple_of(row * block, block)
        pltpu.make_async_copy(kl, kl, sems.at[2]).wait()
        ql = q_ref[pl.ds(base, block), :]
        for g in range(groups):
            k = kl[:, :, g * HD:(g + 1) * HD].reshape(full, HD)
            sl_ref[g * per:(g + 1) * per, :] = lax.dot_general(
                ql[g * per:(g + 1) * per].astype(BF16), k, NT, preferred_element_type=F32
            ) * scale
        nkl = nk_ref[pl.ds(row * groups, groups), :]
        nvl = nv_ref[pl.ds(row * groups, groups), :]
        nkl = jnp.broadcast_to(nkl[:, None, :], (groups, per, HD)).reshape(block, HD)
        nvl = jnp.broadcast_to(nvl[:, None, :], (groups, per, HD)).reshape(block, HD)
        mine = jnp.sum(ql * nkl, axis=1, keepdims=True) * scale
        live = lax.broadcasted_iota(jnp.int32, (block, full), 1) < lengths[row]
        s = jnp.where(live, sl_ref[...], -1e30)
        top = jnp.maximum(jnp.max(s, axis=1, keepdims=True), mine)
        e = jnp.where(live, jnp.exp(s - top), 0.0)
        own_e = jnp.exp(mine - top)
        inv = 1.0 / (jnp.sum(e, axis=1, keepdims=True) + own_e)
        sl_ref[...] = e * inv
        added = (own_e * inv).astype(BF16).astype(F32) * nvl
        pltpu.make_async_copy(vl, vl, sems.at[3]).wait()
        parts = []
        for g in range(groups):
            v = vl[:, :, g * HD:(g + 1) * HD].reshape(full, HD)
            parts.append(jnp.dot(
                sl_ref[g * per:(g + 1) * per, :].astype(BF16), v, preferred_element_type=F32
            ))
        o_ref[pl.ds(base, block), :] = jnp.concatenate(parts, axis=0) + added

    half = heads // 2
    for i in range(half):
        both = [o_ref[pl.ds(j * half + i, reqs, stride=heads), :] for j in range(2)]
        out_ref[:, i * HD:(i + 1) * HD] = jnp.concatenate(both, axis=0).astype(BF16)


def attend(queries, new_key, new_value, keys, values, lengths, table):
    reqs, slots = table.shape
    _, page, width = keys.shape
    groups = width // HD
    short = min(4, slots)
    rows = queries.shape[1] // HD * reqs
    per_req = rows // reqs
    smem = pl.BlockSpec(memory_space=pltpu.SMEM)
    vmem = pl.BlockSpec(memory_space=pltpu.VMEM)
    hbm = pl.BlockSpec(memory_space=pl.ANY)
    return pl.pallas_call(
        functools.partial(attend_kernel, short),
        out_shape=jax.ShapeDtypeStruct((2 * reqs, queries.shape[1] // 2), BF16),
        in_specs=[smem, smem, vmem, vmem, vmem, hbm, hbm],
        out_specs=vmem,
        scratch_shapes=[
            pltpu.VMEM((rows, HD), F32),
            pltpu.VMEM((reqs * groups, HD), F32),
            pltpu.VMEM((reqs * groups, HD), F32),
            pltpu.VMEM((reqs, short, page, width), BF16),
            pltpu.VMEM((reqs, short, page, width), BF16),
            pltpu.VMEM((slots, page, width), BF16),
            pltpu.VMEM((slots, page, width), BF16),
            pltpu.VMEM((rows, short * page), F32),
            pltpu.VMEM((per_req, slots * page), F32),
            pltpu.VMEM((rows, HD), F32),
            pltpu.SemaphoreType.DMA((4,)),
        ],
        compiler_params=pltpu.CompilerParams(vmem_limit_bytes=62 * 2**20),
        name="attend",
    )(
        lengths, table, queries, new_key, new_value, keys, values,
    )


def layer_kernel(
    A, B, att_ref, res_ref, wo_hbm, wg_hbm, wu_hbm, wd_hbm, out_ref,
    wo, wg, wu, wd, att, mix, acc_g, acc_u, xs, xr, hid, pf, ps, r1, zs, r2,
    wsem, sa, ra, sb, rb, ss, rs, sma, rma, smb, rmb, sx, rx, s1, g1, s2, g2,
):
    h = lax.axis_index("head")
    idx = lax.axis_index("req")
    a, b = idx // B, lax.rem(idx, B)
    n = A * B
    rows, c = res_ref.shape
    reqs = att_ref.shape[0] // 2
    kh = att_ref.shape[1]
    tiles, _, tile = acc_g.shape

    def far(da):
        return {"req": lax.rem(a + da, A) * B + b}

    def near(db):
        return {"req": a * B + lax.rem(b + db, B)}

    sibling = {"head": 1 - h}

    loads = [
        pltpu.make_async_copy(x, y, wsem.at[i])
        for i, (x, y) in enumerate(((wo_hbm, wo), (wg_hbm, wg), (wu_hbm, wu), (wd_hbm, wd)))
    ]
    for l in loads:
        l.start()

    barrier = pltpu.get_barrier_semaphore()
    for peer in [far(i) for i in range(1, A)] + [near(i) for i in range(1, B)] + [sibling]:
        pl.semaphore_signal(barrier, inc=1, device_id=peer, device_id_type=MESH)
    att[0, idx] = att_ref[...]
    pl.semaphore_wait(barrier, A + B - 1)

    def send(src, dst, s, r, to):
        cp = pltpu.make_async_remote_copy(
            src_ref=src, dst_ref=dst, send_sem=s, recv_sem=r, device_id=to, device_id_type=MESH
        )
        cp.start()
        return cp

    def source(da, db):
        return lax.rem(a + A - da, A) * B + lax.rem(b + B - db, B)

    def plane(kind):
        return a * B + (b + 1 - 2 * lax.rem(b, 2), b + 2 - 4 * (b // 2), B - 1 - b)[kind]

    def source_plane(da, kind):
        return lax.rem(a + A - da, A) * B + plane(kind) - a * B

    sent = []

    class Gather:
        def __init__(self, ref, sems, cut):
            self.ref, self.sems, self.cut = ref, sems, cut
            self.near, self.part = {}, {}
            self.far = [None] + [
                self.go(ref.at[idx], (0, d), far(d)) for d in range(1, A)
            ]

        def go(self, src, at, to):
            sfar, rfar, snear, rnear = self.sems
            where = (sfar.at[at[1]], rfar.at[at[1]]) if at[0] == 0 else (
                snear.at[at[1:]], rnear.at[at[1:]])
            cp = send(src, src, *where, to)
            sent.append(cp)
            return cp

        def spread(self, da):
            if da:
                self.far[da].wait_recv()
            src = self.ref.at[source(da, 0)]
            if B == 4:
                for kind in range(2):
                    self.near[da, kind] = self.go(src, (1, da, kind), {"req": plane(kind)})
            else:
                for db in range(1, B):
                    self.near[da, db] = self.go(src, (1, da, db), near(db))

        def relay(self, da):
            if B == 4:
                for kind in range(2):
                    self.near[da, kind].wait_recv()
                    src = self.cut(source_plane(da, kind), kind)
                    self.part[da, kind] = self.go(
                        src, (1, da, 2 + kind), {"req": plane(1 - kind)}
                    )
                return [source_plane(da, kind) for kind in range(2)]
            for db in range(1, B):
                self.near[da, db].wait_recv()
            return [source(da, db) for db in range(1, B)]

        def finish(self, da):
            if B == 4:
                for kind in range(2):
                    self.part[da, kind].wait_recv()
                return [source_plane(da, 2)]
            return []

    forwards = {}

    def forward(da, where):
        for at in where:
            i = sum(k[0] == da for k in forwards)
            forwards[da, i] = send(
                att.at[0, at], att.at[1, at], ss.at[da, i], rs.at[da, i], sibling
            )

    first = Gather(
        att.at[0], (sa, ra, sb, rb),
        lambda at, i: att.at[0, at, :, i * (kh // 2):(i + 1) * (kh // 2)],
    )
    for da in range(A):
        first.spread(da)
        forward(da, [source(da, 0)])
        if da:
            forward(da - 1, first.relay(da - 1))
        if da > 1:
            forward(da - 2, first.finish(da - 2))
    forward(A - 1, first.relay(A - 1))
    for da in range(max(A - 2, 0), A):
        forward(da, first.finish(da))

    loads[0].wait()

    def project(slot, side):
        total = None
        lhs = att[slot].reshape(n * 2 * reqs, kh)
        for j in range(2):
            w = wo[pl.ds(pl.multiple_of((side * 2 + j) * kh, kh), kh), :]
            r = jnp.dot(lhs, w, preferred_element_type=F32)
            r = r.reshape(n, 2 * reqs, c)[:, j * reqs:(j + 1) * reqs].reshape(n * reqs, c)
            total = r if total is None else total + r
        return total

    update = project(0, h)
    for cp in forwards.values():
        cp.wait_recv()
    update = update + project(1, 1 - h)
    mix[idx] = (res_ref[...].astype(F32) + update).astype(BF16)

    second = Gather(
        mix, (sma, rma, smb, rmb),
        lambda at, i: mix.at[at, i * (rows // 2):(i + 1) * (rows // 2), :],
    )
    second.spread(0)
    if A > 1:
        second.spread(1)
    second.relay(0)
    loads[1].wait()
    loads[2].wait()
    second.finish(0)
    for da in range(A):
        group = lax.rem(a + A - da, A) * B

        def do_tile(t, carry, da=da, group=group):
            cols = pl.ds(pl.multiple_of(t * tile, tile), tile) if tiles > 1 else slice(None)
            g = u = None
            for k in range(B):
                lhs = mix[group + k]
                at = pl.ds(pl.multiple_of((group + k) * c, c), c)
                gk = jnp.dot(lhs, wg[at, cols], preferred_element_type=F32)
                uk = jnp.dot(lhs, wu[at, cols], preferred_element_type=F32)
                g = gk if g is None else g + gk
                u = uk if u is None else u + uk
            if da:
                g = g + acc_g[t]
                u = u + acc_u[t]
            acc_g[t] = g
            acc_u[t] = u
            if da == A - 1:
                xs[t, 0] = g.astype(BF16)
                xs[t, 1] = u.astype(BF16)
                send(xs.at[t], xr.at[t], sx.at[t], rx.at[t], sibling)
            return carry

        middle = (tiles + 1) // 2
        lax.fori_loop(0, middle, do_tile, 0)
        if da + 1 < A:
            second.relay(da + 1)
        if da + 2 < A:
            second.spread(da + 2)
        lax.fori_loop(middle, tiles, do_tile, 0)
        if da + 1 < A:
            second.finish(da + 1)

    for t in range(tiles):
        pltpu.make_async_remote_copy(
            src_ref=xs.at[t], dst_ref=xr.at[t], send_sem=sx.at[t], recv_sem=rx.at[t],
            device_id=sibling, device_id_type=MESH,
        ).wait()
        g = acc_g[t] + xr[t, 0].astype(F32)
        u = acc_u[t] + xr[t, 1].astype(F32)
        hid[:, t * tile:(t + 1) * tile] = (g / (1.0 + jnp.exp(-g)) * u).astype(BF16)

    loads[3].wait()
    width = max(c, min(256, B * c))
    inner = width // c
    firsts, seconds = {}, []

    def reduce(i):
        total = pf[i % 2, b]
        for db in range(1, B):
            firsts[i, db].wait_recv()
            total = total + r1[i, db].astype(F32)
        return total

    def pass_on(i):
        zs[i] = reduce(i).astype(BF16)
        seconds.append(send(zs.at[i], r2.at[i], s2.at[i], g2.at[i], far(i + 1)))

    for i in range(A):
        ta = lax.rem(a + 1 + i, A)

        def do_cols(k, carry, i=i, ta=ta):
            cols = pl.ds(pl.multiple_of(ta * (B * c) + k * width, width), width)
            r = jnp.dot(hid[...], wd[:, cols], preferred_element_type=F32)
            for m in range(inner):
                piece = r[:, m * c:(m + 1) * c]
                pf[i % 2, k * inner + m] = piece
                ps[i, k * inner + m] = piece.astype(BF16)
            return carry

        lax.fori_loop(0, B // inner, do_cols, 0)
        for db in range(1, B):
            firsts[i, db] = send(
                ps.at[i, lax.rem(b + db, B)], r1.at[i, db], s1.at[i, db], g1.at[i, db], near(db)
            )
        if i:
            pass_on(i - 1)
    total = mix[idx].astype(F32) + reduce(A - 1)
    for i, cp in enumerate(seconds):
        cp.wait_recv()
        total = total + r2[i].astype(F32)
    out_ref[...] = total.astype(BF16)

    for cp in sent + list(forwards.values()) + list(firsts.values()) + seconds:
        cp.wait_send()


def layer(n, att, residual, wo, wg, wu, wd):
    A = 4 if n % 4 == 0 else 1
    B = n // A
    rows, c = residual.shape
    ff = wg.shape[1]
    tile = 256 if ff % 256 == 0 else ff
    tiles = ff // tile
    vmem = pl.BlockSpec(memory_space=pltpu.VMEM)
    hbm = pl.BlockSpec(memory_space=pl.ANY)
    dma = pltpu.SemaphoreType.DMA
    return pl.pallas_call(
        functools.partial(layer_kernel, A, B),
        out_shape=jax.ShapeDtypeStruct((rows, c), BF16),
        in_specs=[vmem, vmem, hbm, hbm, hbm, hbm],
        out_specs=vmem,
        scratch_shapes=[
            pltpu.VMEM(wo.shape, BF16),
            pltpu.VMEM(wg.shape, BF16),
            pltpu.VMEM(wu.shape, BF16),
            pltpu.VMEM(wd.shape, BF16),
            pltpu.VMEM((2, n) + att.shape, BF16),
            pltpu.VMEM((n, rows, c), BF16),
            pltpu.VMEM((tiles, rows, tile), F32),
            pltpu.VMEM((tiles, rows, tile), F32),
            pltpu.VMEM((tiles, 2, rows, tile), BF16),
            pltpu.VMEM((tiles, 2, rows, tile), BF16),
            pltpu.VMEM((rows, ff), BF16),
            pltpu.VMEM((2, B, rows, c), F32),
            pltpu.VMEM((A, B, rows, c), BF16),
            pltpu.VMEM((A, B, rows, c), BF16),
            pltpu.VMEM((A, rows, c), BF16),
            pltpu.VMEM((A, rows, c), BF16),
            dma((4,)),
            dma((A,)), dma((A,)), dma((A, B)), dma((A, B)), dma((A, B)), dma((A, B)),
            dma((A,)), dma((A,)), dma((A, B)), dma((A, B)),
            dma((tiles,)), dma((tiles,)),
            dma((A, B)), dma((A, B)), dma((A,)), dma((A,)),
        ],
        compiler_params=pltpu.CompilerParams(
            vmem_limit_bytes=63 * 2**20, collective_id=0, has_side_effects=True
        ),
        name="layer",
    )(att, residual, wo, wg, wu, wd)


def solution(mesh):
    n = mesh.shape["req"]

    def body(
        queries, new_key, new_value, key_cache, value_cache, lengths, page_table,
        residual, out_weight, gate_weight, up_weight, down_weight,
    ):
        att = attend(queries, new_key, new_value, key_cache, value_cache, lengths, page_table)
        return layer(n, att, residual, out_weight, gate_weight, up_weight, down_weight)

    return jax.shard_map(
        body,
        mesh=mesh,
        in_specs=(
            P("req", "head"),
            P("req", "head"),
            P("req", "head"),
            P("req", None, "head"),
            P("req", None, "head"),
            P("req"),
            P("req", None),
            P(None, ("head", "req")),
            P(None, ("head", "req")),
            P("head", "req"),
            P("head", "req"),
            P("req", "head"),
        ),
        out_specs=P(None, ("head", "req")),
        check_vma=False,
    )
```
